32 devices in a mesh: rep: 2 (over y), gx: 4 (over z), gy: 4 (over x, core).
Axes of the slice: x: 2, y: 2, z: 4, core: 2. Of those that a mesh axis runs over, the one named last changes fastest.
Arguments:
- normed: bfloat16 [4, 256, 8192], P(None, 'rep', ('gy', 'gx')), parts along dimension 1, may hold values from -6 to 6
- in_weight: bfloat16 [2, 8192, 16384], P(None, 'gy', 'gx'), may hold values from -0.0625 to 0.0625
- conv_weight: float32 [4, 16384], P(None, ('gx', 'gy')), may hold values from -0.8 to 0.8
- conv_bias: float32 [16384], P(('gx', 'gy')), may hold values from -0.8 to 0.8
- x_weight: bfloat16 [16384, 544], P(('gx', 'gy')), may hold values from -0.046875 to 0.046875
- dt_weight: bfloat16 [512, 16384], P(None, ('gx', 'gy')), may hold values from -0.25 to 0.25
- dt_bias: float32 [16384], P(('gx', 'gy')), may hold values from -5 to -0.5
- a_log: float32 [16, 16384], P(None, ('gx', 'gy')), may hold values from 0 to 2.77
- skip: float32 [16384], P(('gx', 'gy')), may hold values from 0.5 to 2
- conv_state: bfloat16 [3, 256, 16384], P(None, 'rep', ('gx', 'gy')), parts along dimension 1, may hold values from -6 to 6
- ssm_state: float32 [256, 16, 16384], P('rep', None, ('gx', 'gy')), parts along dimension 0, may hold values from -6 to 6
- out_weight: bfloat16 [16384, 8192], P('gx', 'gy'), may hold values from -0.046875 to 0.046875
Outputs:
- mixed: bfloat16 [4, 256, 8192], P(None, 'rep', ('gy', 'gx')), parts along dimension 1
- conv_next: bfloat16 [3, 256, 16384], P(None, 'rep', ('gx', 'gy')), parts along dimension 1
- ssm_next: float32 [256, 16, 16384], P('rep', None, ('gx', 'gy')), parts along dimension 0
The draws below stay inside these ranges and needn't reach their ends.
There are 2 independent parts, one for each index of `rep`. The reference program is written for one: setup_inputs(seed, part) draws one part's arguments, and reference() takes and returns one part's arrays. A program takes and returns all parts, laid end to end along the dimension named above; an argument that names none is the same for every part. Nothing has to cross between parts.
All inputs are finite; a program needn't handle non-finite values.
Results may differ from the reference program's by a relative error of at most 0.02.
Values may be sent and summed in bfloat16 or wider, within the bound.
No kernel may reach another device: no remote copies, remote signals or barrier semaphores. Data moves between devices by JAX's collectives and lax.ppermute only.
A program may use at most 192 MiB of HBM per device.

```python
import jax
import jax.numpy as jnp
from jax import lax

D = 8192
E = 16384
N = 16
CONV = 4
DT = 512
ROWS = 128
STEPS = 4
XW = 544
N_GY = 4


def steps_of(rng, shape, shards, low, largest):
    def one(dim, parts):
        steps = jax.random.uniform(jax.random.fold_in(jax.random.fold_in(rng, 6), dim), (parts,), jnp.float32, low / len(shards), largest / len(shards))
        return jnp.repeat(jnp.exp(steps), shape[dim] // parts).reshape((-1,) + (1,) * (len(shape) - dim - 1))

    gain = one(*shards[0])
    for cut in shards[1:]:
        gain = gain * one(*cut)
    return gain


def gaussian(rng, dims, scale, bound, pieces=(), held_as=jnp.bfloat16):
    level = steps_of(rng, dims, pieces, -0.22, 0.18) if pieces else 1.0
    values = jax.random.normal(rng, dims, jnp.float32) * scale * level
    return jnp.minimum(jnp.maximum(values, -bound), bound).astype(held_as)


def setup_inputs(seed: int = 0, part: int = 0) -> dict:
    key_list = jax.random.split(jax.random.key(seed), 13)
    part_keys = jax.random.split(jax.random.fold_in(key_list[12], part), 13)
    normed = gaussian(part_keys[0], (STEPS, ROWS, D), 1.0, 6.0, ((2, 16),))
    in_weight = gaussian(key_list[1], (2, D, E), D ** -0.5, 0.0625, ((1, 4), (2, 4)))
    conv_weight = jnp.clip(jax.random.uniform(key_list[2], (CONV, E), jnp.float32, -0.8, 0.8) * steps_of(key_list[2], (CONV, E), ((1, 16),), -0.4, 0.0), -0.8, 0.8)
    conv_bias = jnp.clip(jax.random.uniform(key_list[3], (E,), jnp.float32, -0.8, 0.8) * steps_of(key_list[3], (E,), ((0, 16),), -0.4, 0.0), -0.8, 0.8)
    x_weight = gaussian(key_list[4], (E, XW), E ** -0.5, 0.046875, ((0, 16),))
    dt_weight = gaussian(key_list[5], (DT, E), DT ** -0.5, 0.25, ((1, 16),))
    dt_bias = jnp.clip(-5.0 + 4.5 * jax.random.uniform(key_list[6], (E,), jnp.float32) ** steps_of(key_list[6], (E,), ((0, 16),), -0.2, 0.2), -5.0, -0.5)
    a_log = jnp.clip(2.77 * jax.random.uniform(key_list[7], (N, E), jnp.float32) ** steps_of(key_list[7], (N, E), ((1, 16),), -0.2, 0.2), 0.0, 2.77)
    skip = jnp.clip(0.5 + 1.5 * jax.random.uniform(key_list[8], (E,), jnp.float32) ** steps_of(key_list[8], (E,), ((0, 16),), -0.2, 0.2), 0.5, 2.0)
    conv_state = gaussian(part_keys[9], (CONV - 1, ROWS, E), 1.0, 6.0, ((2, 16),))
    ssm_state = gaussian(part_keys[10], (ROWS, N, E), 1.0, 6.0, ((2, 16),), jnp.float32)
    out_weight = gaussian(key_list[11], (E, D), E ** -0.5, 0.046875, ((0, 4), (1, 4)))
    return dict(normed=normed, in_weight=in_weight, conv_weight=conv_weight, conv_bias=conv_bias, x_weight=x_weight, dt_weight=dt_weight, dt_bias=dt_bias, a_log=a_log, skip=skip, conv_state=conv_state, ssm_state=ssm_state, out_weight=out_weight)


def reference(normed, in_weight, conv_weight, conv_bias, x_weight, dt_weight, dt_bias, a_log, skip, conv_state, ssm_state, out_weight):
    width = D // N_GY
    a_rate = -jnp.exp(a_log)
    conv = conv_state
    state = ssm_state
    outputs = []
    for position in range(STEPS):
        token_rows = normed[position]

        def add_block(totals, index):
            offset = (index * width).astype(jnp.int32)
            piece = lax.dynamic_slice_in_dim(token_rows, offset, width, 1)
            rows_inner = lax.dynamic_slice_in_dim(in_weight[0], offset, width, 0)
            rows_gate = lax.dynamic_slice_in_dim(in_weight[1], offset, width, 0)
            part_inner = jnp.dot(piece, rows_inner, preferred_element_type=jnp.float32).astype(jnp.bfloat16)
            part_gate = jnp.dot(piece, rows_gate, preferred_element_type=jnp.float32).astype(jnp.bfloat16)
            part_inner, part_gate = lax.optimization_barrier((part_inner, part_gate))
            return (totals[0] + part_inner.astype(jnp.float32), totals[1] + part_gate.astype(jnp.float32)), None

        empty = jnp.zeros((ROWS, E), jnp.float32)
        (sum_inner, sum_gate), _ = lax.scan(add_block, (empty, empty), jnp.arange(N_GY, dtype=jnp.int32))
        inner_input = sum_inner.astype(jnp.bfloat16)
        gate_input = sum_gate.astype(jnp.bfloat16)
        accum = conv_bias[None, :] + conv_weight[CONV - 1][None, :] * inner_input.astype(jnp.float32)
        for tap in range(CONV - 1):
            accum = accum + conv_weight[tap][None, :] * conv[tap].astype(jnp.float32)
        conv_out = jax.nn.silu(accum).astype(jnp.bfloat16)
        conv = jnp.concatenate([conv[1:], inner_input[None]], axis=0)
        proj = jnp.dot(conv_out, x_weight, preferred_element_type=jnp.float32)
        step_low = proj[:, :DT].astype(jnp.bfloat16)
        b_in = proj[:, DT:DT + N]
        c_out = proj[:, DT + N:]
        delta = jax.nn.softplus(jnp.dot(step_low, dt_weight, preferred_element_type=jnp.float32) + dt_bias[None, :])
        conv_float = conv_out.astype(jnp.float32)
        state = jnp.exp(delta[:, None, :] * a_rate[None, :, :]) * state + delta[:, None, :] * b_in[:, :, None] * conv_float[:, None, :]
        result = jnp.sum(c_out[:, :, None] * state, axis=1) + skip[None, :] * conv_float
        gated = (result * jax.nn.silu(gate_input.astype(jnp.float32))).astype(jnp.bfloat16)
        outputs.append(jnp.dot(gated, out_weight, preferred_element_type=jnp.float32).astype(jnp.bfloat16))
    return jnp.stack(outputs, axis=0), conv, state
```

```python
import functools

import jax
import jax.numpy as jnp
from jax import lax
from jax.experimental import pallas as pl
from jax.experimental.pallas import tpu as pltpu
from jax.sharding import PartitionSpec as P

N = 16
CONV = 4
DT = 512
CHUNKS = 2
LOG2E = 1.4426950408889634
BF = jnp.bfloat16
F32 = jnp.float32
IN_VMEM = pl.BlockSpec(memory_space=pltpu.VMEM)
ANYWHERE = pl.BlockSpec(memory_space=pl.ANY)
SCALARS = pl.BlockSpec(memory_space=pltpu.SMEM)


def _params(mib):
    return pltpu.CompilerParams(vmem_limit_bytes=mib * 1024 * 1024)


def _load_kernel(half, source, _, target, sem):
    copy = pltpu.make_async_copy(source if half is None else source.at[half], target, sem)
    copy.start()
    copy.wait()


def load(weight, half, after):
    return pl.pallas_call(
        functools.partial(_load_kernel, half),
        out_shape=jax.ShapeDtypeStruct(weight.shape[-2:], weight.dtype),
        in_specs=[ANYWHERE] * 2,
        out_specs=IN_VMEM,
        scratch_shapes=[pltpu.SemaphoreType.DMA],
        compiler_params=_params(8),
        name="load",
    )(weight, after)


def _in_kernel(sibling, place, *refs):
    *pieces, weight, _, out = refs
    depth = pieces[0].shape[1]
    channels = out.shape[2]
    core = jnp.bitwise_xor(jnp.bitwise_and(place[1], 1), sibling)
    for i in range(2):
        chip = jnp.bitwise_xor(jnp.right_shift(place[1], 1), 1 - i)
        columns = pl.ds(pl.multiple_of((chip * 2 + core) * channels, channels), channels)
        total = None
        for k, piece in enumerate(pieces):
            start = pl.multiple_of(jnp.bitwise_xor(place[0], k) * depth, depth)
            part = jnp.dot(
                piece[...], weight[pl.ds(start, depth), columns], preferred_element_type=F32
            )
            total = part if total is None else total + part
        out[i] = total.astype(out.dtype)


def in_proj(place, pieces, weight, sibling, after):
    rows = pieces[0].shape[0]
    channels = weight.shape[1] // 4
    return pl.pallas_call(
        functools.partial(_in_kernel, sibling),
        out_shape=jax.ShapeDtypeStruct((2, rows, channels), BF),
        in_specs=[SCALARS] + [IN_VMEM] * (len(pieces) + 1) + [ANYWHERE],
        out_specs=IN_VMEM,
        compiler_params=_params(8),
        name="in_proj",
    )(place, *pieces, weight, after)


def _out_kernel(place, g0, g1, g2, g3, weight, *outs):
    channels = g0.shape[1]
    width = outs[0].shape[1]
    for i, out in enumerate(outs):
        target = jnp.bitwise_xor(place[0], 3 - i)
        columns = pl.ds(pl.multiple_of(target * width, width), width)
        total = None
        for k, piece in enumerate((g0, g1, g2, g3)):
            start = pl.multiple_of(jnp.bitwise_xor(place[1], k) * channels, channels)
            part = jnp.dot(
                piece[...], weight[pl.ds(start, channels), columns], preferred_element_type=F32
            )
            total = part if total is None else total + part
        out[...] = total.astype(out.dtype)


def out_proj(place, pieces, out_weight):
    rows = pieces[0].shape[0]
    width = out_weight.shape[1] // 4
    return pl.pallas_call(
        _out_kernel,
        out_shape=[jax.ShapeDtypeStruct((rows, width), BF)] * 4,
        in_specs=[SCALARS] + [IN_VMEM] * 5,
        out_specs=[IN_VMEM] * 4,
        compiler_params=_params(8),
        name="out_proj",
    )(place, *pieces, out_weight)


def _ssm_kernel(
    steps, low, bc, conv_out, gate, dt_weight, dt_bias, skip, a_log, state, _, new_state, gated,
    delta, conv, result, spread
):
    batch = low.shape[0] // steps
    width = gate.shape[1]

    @pl.when(pl.program_id(0) == 0)
    def _():
        for group in range(steps * batch // 8):
            some = bc[group * 8 : group * 8 + 8, :]
            for n in range(2 * N):
                spread[group * 2 * N + n] = jnp.broadcast_to(some[:, n : n + 1], (8, width))

    delta[...] = jax.nn.softplus(
        jnp.dot(low[...], dt_weight[...], preferred_element_type=F32) + dt_bias[...]
    )
    conv[...] = conv_out[...].astype(F32)
    rate = jnp.exp(a_log[...]) * (-LOG2E)

    def rows_of(block, carry):
        first = pl.multiple_of(block * 8, 8)
        d, dx, acc = [], [], []
        for t in range(steps):
            here = pl.ds(t * batch + first, 8)
            d.append(delta[here, :])
            dx.append(d[t] * conv[here, :])
            acc.append(None)
        for n in range(N):
            rows = pl.ds(first * N + n, 8, stride=N)
            s = state[rows, :]
            a = jnp.broadcast_to(rate[n : n + 1, :], (8, width))
            for t in range(steps):
                group = (t * (batch // 8) + block) * 2 * N
                s = jnp.exp2(d[t] * a) * s + dx[t] * spread[group + n]
                y = spread[group + N + n] * s
                acc[t] = y if acc[t] is None else acc[t] + y
            new_state[rows, :] = s
        for t in range(steps):
            result[pl.ds(t * batch + first, 8), :] = acc[t]
        return carry

    lax.fori_loop(0, batch // 8, rows_of, 0)
    gate_float = gate[...].astype(F32)
    gated[...] = (
        (result[...] + skip[...] * conv[...]) * (gate_float * jax.nn.sigmoid(gate_float))
    ).astype(gated.dtype)


def ssm(chunk, steps, low, bc, conv_out, gate, dt_weight, dt_bias, skip, a_log, state, carry, tile=128):
    rows, channels = conv_out.shape
    tile = min(tile, channels)
    batch = rows // steps
    kernel = functools.partial(_ssm_kernel, steps)
    state_spec = pl.BlockSpec((batch * N, tile), lambda j: (chunk, j))
    column = lambda count: pl.BlockSpec((count, tile), lambda j: (0, j))
    whole = lambda array: pl.BlockSpec(array.shape, lambda j: (0, 0))
    args = [low, bc, conv_out, gate, dt_weight, dt_bias, skip, a_log, state]
    in_specs = [
        whole(low), whole(bc), column(rows), column(rows), column(DT), column(1), column(1),
        column(N), state_spec,
    ]
    aliases = {}
    if carry is None:
        kernel_fn = lambda *refs: kernel(*refs[:9], None, *refs[9:])
    else:
        args.append(carry)
        in_specs.append(pl.BlockSpec(memory_space=pl.ANY))
        aliases = {9: 0}
        kernel_fn = kernel
    return pl.pallas_call(
        kernel_fn,
        out_shape=[
            jax.ShapeDtypeStruct(state.shape, F32),
            jax.ShapeDtypeStruct((rows, channels), BF),
        ],
        grid=(channels // tile,),
        in_specs=in_specs,
        out_specs=[state_spec, column(rows)],
        scratch_shapes=[pltpu.VMEM((rows, tile), F32)] * 3
        + [pltpu.VMEM((rows // 8 * 2 * N, 8, tile), F32)],
        input_output_aliases=aliases,
        compiler_params=_params(10),
        name="ssm",
    )(*args)


def _swap(array, axis, size, bits):
    return lax.ppermute(array, axis, [(i, i ^ bits) for i in range(size)])


def _core(array):
    return _swap(array, "gy", 4, 1)


def _chip(array):
    return _swap(array, "gy", 4, 2)


def _gx(array, bits):
    return _swap(array, "gx", 4, bits)


def _order(array, *earlier):
    return lax.optimization_barrier((array, *earlier))[0]


def _add(*arrays):
    return functools.reduce(jnp.add, [a.astype(F32) for a in arrays])


def chunked(
    normed, in_weight, conv_weight, conv_bias, x_weight, dt_weight, dt_bias, a_log, skip,
    conv_state, ssm_state, out_weight
):
    steps, batch, depth = normed.shape
    channels = conv_bias.shape[0]
    gy = lax.axis_index("gy")
    place = jnp.stack([lax.axis_index("gx"), gy]).astype(jnp.int32)
    core = gy & 1
    flat_state = ssm_state.reshape(batch * N, channels)
    piece = batch // CHUNKS
    rows = steps * piece
    chunks = range(CHUNKS)
    cut = [slice(c * piece, (c + 1) * piece) for c in chunks]

    weights = [load(in_weight, 0, place)]
    weights.append(load(in_weight, 1, weights[0]))
    gathered = []
    before = None
    for c in chunks:
        own = normed[:, cut[c], :].reshape(rows, depth)
        if before is not None:
            own = _order(own, before)
        two = _gx(own, 2)
        one = _gx(own, 1)
        relay = _order(two, weights[c])
        gathered.append((own, one, two, _gx(relay, 1)))
        before = relay

    arrived = {}
    after = weights[1]
    for half in range(2):
        for c in chunks:
            pieces = (_order(gathered[c][0], after),) + gathered[c][1:]
            away = in_proj(place, pieces, weights[half], 1, after)
            near = _core(away)
            kept = in_proj(place, pieces, weights[half], 0, away)
            summed = _add(kept[0], near[0]).astype(BF)
            after = summed
            arrived[half, c] = _add(kept[1], near[1], _chip(summed)).astype(BF)
    out_copy = load(out_weight, None, after)

    carry = None
    conv_pieces, outputs = [], []
    for c in chunks:
        inner = arrived[0, c].reshape(steps, piece, channels)
        history = jnp.concatenate([conv_state[:, cut[c], :], inner], axis=0).astype(F32)
        accum = conv_bias[None, None, :]
        for tap in range(CONV):
            accum = accum + conv_weight[tap][None, None, :] * history[tap : tap + steps]
        conv_out = jax.nn.silu(accum).astype(BF).reshape(rows, channels)
        conv_pieces.append(inner[steps - CONV + 1 :])

        proj = jnp.dot(conv_out, x_weight, preferred_element_type=F32)
        half_rows = rows // 2
        theirs = lax.dynamic_slice_in_dim(proj, (1 - core) * half_rows, half_rows, 0)
        mine = lax.dynamic_slice_in_dim(proj, core * half_rows, half_rows, 0)
        mine = _add(mine, _core(theirs.astype(BF)))
        mine = _add(mine, _chip(mine.astype(BF)))
        mine = _add(mine, _gx(mine.astype(BF), 1))
        mine = _add(mine, _gx(mine.astype(BF), 2)).astype(BF)
        sibling = _core(mine)
        both = jnp.where(
            core == 0,
            jnp.concatenate([mine, sibling], axis=0),
            jnp.concatenate([sibling, mine], axis=0),
        )
        low = both[:, :DT]
        b_c = both[:, DT:].astype(F32)

        carry, gated = ssm(
            c, steps, low, b_c, conv_out, arrived[1, c], dt_weight, dt_bias[None, :],
            skip[None, :], a_log, flat_state, carry,
        )
        across = _chip(gated)
        three, two, one, own = out_proj(
            place, (gated, _core(gated), across, _core(across)), out_copy
        )
        joined = _add(two, _gx(three, 1)).astype(BF)
        outputs.append(
            _add(own, _gx(one, 1), _gx(joined, 2)).astype(BF).reshape(steps, piece, depth)
        )
    return (
        jnp.concatenate(outputs, axis=1),
        jnp.concatenate(conv_pieces, axis=1),
        carry.reshape(ssm_state.shape),
    )


def per_device(
    normed,
    in_weight,
    conv_weight,
    conv_bias,
    x_weight,
    dt_weight,
    dt_bias,
    a_log,
    skip,
    conv_state,
    ssm_state,
    out_weight,
):
    a_rate = -jnp.exp(a_log)
    conv = conv_state
    state = ssm_state
    outputs = []
    for position in range(normed.shape[0]):
        partial_value = jnp.einsum(
            "rd,hde->rhe",
            lax.all_gather(normed[position], "gx", axis=1, tiled=True),
            in_weight,
            preferred_element_type=jnp.float32,
        )
        both_halves = lax.psum_scatter(
            partial_value.astype(jnp.bfloat16), "gy", scatter_dimension=2, tiled=True
        )
        inner_input = both_halves[:, 0, :]
        gate_input = both_halves[:, 1, :]
        accum = conv_bias[None, :] + conv_weight[CONV - 1][None, :] * inner_input.astype(
            jnp.float32
        )
        for tap in range(CONV - 1):
            accum = accum + conv_weight[tap][None, :] * conv[tap].astype(jnp.float32)
        conv_out = jax.nn.silu(accum).astype(jnp.bfloat16)
        conv = jnp.concatenate([conv[1:], inner_input[None]], axis=0)
        proj = lax.psum(
            jnp.dot(conv_out, x_weight, preferred_element_type=jnp.float32), ("gx", "gy")
        )
        step_low = proj[:, :DT].astype(jnp.bfloat16)
        b_in = proj[:, DT : DT + N]
        c_out = proj[:, DT + N :]
        delta = jax.nn.softplus(
            jnp.dot(step_low, dt_weight, preferred_element_type=jnp.float32) + dt_bias[None, :]
        )
        conv_float = conv_out.astype(jnp.float32)
        state = (
            jnp.exp(delta[:, None, :] * a_rate[None, :, :]) * state
            + delta[:, None, :] * b_in[:, :, None] * conv_float[:, None, :]
        )
        result = jnp.sum(c_out[:, :, None] * state, axis=1) + skip[None, :] * conv_float
        gated = (result * jax.nn.silu(gate_input.astype(jnp.float32))).astype(jnp.bfloat16)
        out_partial = jnp.dot(
            lax.all_gather(gated, "gy", axis=1, tiled=True),
            out_weight,
            preferred_element_type=jnp.float32,
        )
        outputs.append(
            lax.psum_scatter(
                out_partial.astype(jnp.bfloat16), "gx", scatter_dimension=1, tiled=True
            )
        )
    return (jnp.stack(outputs, axis=0), conv, state)


def solution(mesh):
    narrow = mesh.shape["gx"] == 4 and mesh.shape["gy"] == 4
    return jax.shard_map(
        chunked if narrow else per_device,
        mesh=mesh,
        in_specs=(
            P(None, "rep", ("gy", "gx")),
            P(None, "gy", "gx"),
            P(None, ("gx", "gy")),
            P(("gx", "gy")),
            P(("gx", "gy"), None),
            P(None, ("gx", "gy")),
            P(("gx", "gy")),
            P(None, ("gx", "gy")),
            P(("gx", "gy")),
            P(None, "rep", ("gx", "gy")),
            P("rep", None, ("gx", "gy")),
            P("gx", "gy"),
        ),
        out_specs=(
            P(None, "rep", ("gy", "gx")),
            P(None, "rep", ("gx", "gy")),
            P("rep", None, ("gx", "gy")),
        ),
        check_vma=False,
    )
```

```python
import functools

import jax
import jax.numpy as jnp
from jax import lax
from jax.experimental import pallas as pl
from jax.experimental.pallas import tpu as pltpu
from jax.sharding import PartitionSpec as P

N = 16
CONV = 4
DT = 512
CHUNKS = 2
LOG2E = 1.4426950408889634
BF = jnp.bfloat16
F32 = jnp.float32
IN_VMEM = pl.BlockSpec(memory_space=pltpu.VMEM)
ANYWHERE = pl.BlockSpec(memory_space=pl.ANY)
IN_HBM = pl.BlockSpec(memory_space=pltpu.HBM)
SCALARS = pl.BlockSpec(memory_space=pltpu.SMEM)


def _params(mib):
    return pltpu.CompilerParams(vmem_limit_bytes=mib * 1024 * 1024)


def _load_kernel(half, source, _, target, sem):
    copy = pltpu.make_async_copy(source if half is None else source.at[half], target, sem)
    copy.start()
    copy.wait()


def load(weight, half, after):
    return pl.pallas_call(
        functools.partial(_load_kernel, half),
        out_shape=jax.ShapeDtypeStruct(weight.shape[-2:], weight.dtype),
        in_specs=[ANYWHERE] * 2,
        out_specs=IN_VMEM,
        scratch_shapes=[pltpu.SemaphoreType.DMA],
        compiler_params=_params(8),
        name="load",
    )(weight, after)


def _in_kernel(sibling, place, *refs):
    *pieces, weight, _, out = refs
    depth = pieces[0].shape[1]
    channels = out.shape[2]
    core = jnp.bitwise_xor(jnp.bitwise_and(place[1], 1), sibling)
    for i in range(2):
        chip = jnp.bitwise_xor(jnp.right_shift(place[1], 1), 1 - i)
        columns = pl.ds(pl.multiple_of((chip * 2 + core) * channels, channels), channels)
        total = None
        for k, piece in enumerate(pieces):
            start = pl.multiple_of(jnp.bitwise_xor(place[0], k) * depth, depth)
            part = jnp.dot(
                piece[...], weight[pl.ds(start, depth), columns], preferred_element_type=F32
            )
            total = part if total is None else total + part
        out[i] = total.astype(out.dtype)


def in_proj(place, pieces, weight, sibling, after):
    rows = pieces[0].shape[0]
    channels = weight.shape[1] // 4
    return pl.pallas_call(
        functools.partial(_in_kernel, sibling),
        out_shape=jax.ShapeDtypeStruct((2, rows, channels), BF),
        in_specs=[SCALARS] + [IN_VMEM] * (len(pieces) + 1) + [ANYWHERE],
        out_specs=IN_VMEM,
        compiler_params=_params(8),
        name="in_proj",
    )(place, *pieces, weight, after)


def _out_kernel(place, g0, g1, g2, g3, weight, *refs):
    *outs, held, sems = refs
    channels = g0.shape[1]
    count, _, width = held.shape
    copies = []
    for i in range(count):
        target = jnp.bitwise_xor(place[0], 3 - i)
        copies.append(
            pltpu.make_async_copy(
                weight.at[:, pl.ds(pl.multiple_of(target * width, width), width)],
                held.at[i],
                sems.at[i],
            )
        )
        copies[i].start()
    for i, out in enumerate(outs):
        copies[i].wait()
        total = None
        for k, piece in enumerate((g0, g1, g2, g3)):
            start = pl.multiple_of(jnp.bitwise_xor(place[1], k) * channels, channels)
            part = jnp.dot(
                piece[...], held[i, pl.ds(start, channels), :], preferred_element_type=F32
            )
            total = part if total is None else total + part
        out[...] = total.astype(out.dtype)


def out_proj(place, pieces, out_weight):
    rows = pieces[0].shape[0]
    width = out_weight.shape[1] // 4
    return pl.pallas_call(
        _out_kernel,
        out_shape=[jax.ShapeDtypeStruct((rows, width), BF)] * 4,
        in_specs=[SCALARS] + [IN_VMEM] * 4 + [IN_HBM],
        out_specs=[IN_VMEM] * 4,
        scratch_shapes=[
            pltpu.VMEM((4, out_weight.shape[0], width), BF),
            pltpu.SemaphoreType.DMA((4,)),
        ],
        compiler_params=_params(50),
        name="out_proj",
    )(place, *pieces, out_weight)


def _ssm_kernel(
    chunk, steps, low, bc, conv_out, dt_weight, dt_bias, skip, a_log, state, _, new_state, mixed,
    held, delta, conv, result, spread, arrive, leave
):
    batch = low.shape[0] // steps
    count, height, lanes = held.shape
    mine = pl.ds(chunk * height, height)
    columns = [pl.ds(j * lanes, lanes) for j in range(count)]
    copies = [
        pltpu.make_async_copy(state.at[mine, columns[j]], held.at[j], arrive.at[j])
        for j in range(count)
    ]
    for copy in copies:
        copy.start()

    for group in range(steps * batch // 8):
        some = bc[group * 8 : group * 8 + 8, :]
        for n in range(2 * N):
            spread[group * 2 * N + n] = jnp.broadcast_to(some[:, n : n + 1], (8, lanes))

    width = delta.shape[1]
    per = width // lanes
    outgoing = []
    for j in range(0, count, per):
        here = slice(j * lanes, j * lanes + width)
        delta[...] = jax.nn.softplus(
            jnp.dot(low[...], dt_weight[:, here], preferred_element_type=F32) + dt_bias[:, here]
        )
        conv[...] = conv_out[:, here].astype(F32)
        rate = jnp.exp(a_log[:, here]) * (-LOG2E)
        for h in range(per):
            copies[j + h].wait()

        def rows_of(block, carry, j=j, rate=rate):
            first = pl.multiple_of(block * 8, 8)
            pairs = [(t, h) for t in range(steps) for h in range(per)]
            d, dx, acc = {}, {}, {}
            for t, h in pairs:
                place = pl.ds(t * batch + first, 8), slice(h * lanes, (h + 1) * lanes)
                d[t, h] = delta[place]
                dx[t, h] = d[t, h] * conv[place]
            for n in range(N):
                rows = pl.ds(first * N + n, 8, stride=N)
                s = [held[j + h, rows, :] for h in range(per)]
                a = [
                    jnp.broadcast_to(rate[n : n + 1, h * lanes : (h + 1) * lanes], (8, lanes))
                    for h in range(per)
                ]
                for t in range(steps):
                    group = (t * (batch // 8) + block) * 2 * N
                    b = spread[group + n]
                    c = spread[group + N + n]
                    for h in range(per):
                        s[h] = jnp.exp2(d[t, h] * a[h]) * s[h] + dx[t, h] * b
                        y = c * s[h]
                        acc[t, h] = y if n == 0 else acc[t, h] + y
                for h in range(per):
                    held[j + h, rows, :] = s[h]
            for t, h in pairs:
                place = pl.ds(t * batch + first, 8), slice(h * lanes, (h + 1) * lanes)
                result[place] = acc[t, h]
            return carry

        lax.fori_loop(0, batch // 8, rows_of, 0)
        for h in range(per):
            copy = pltpu.make_async_copy(
                held.at[j + h], new_state.at[mine, columns[j + h]], leave.at[j + h]
            )
            copy.start()
            outgoing.append(copy)
        mixed[:, here] = result[...] + skip[:, here] * conv[...]
    for copy in outgoing:
        copy.wait()


def ssm(chunk, steps, low, bc, conv_out, dt_weight, dt_bias, skip, a_log, state, carry):
    rows, channels = conv_out.shape
    height = rows // steps * N
    lanes = 128
    count = channels // lanes
    width = 2 * lanes
    kernel = functools.partial(_ssm_kernel, chunk, steps)
    args = [low, bc, conv_out, dt_weight, dt_bias, skip, a_log, state]
    in_specs = [IN_VMEM] * 7 + [IN_HBM]
    aliases = {}
    if carry is None:
        kernel_fn = lambda *refs: kernel(*refs[:8], None, *refs[8:])
    else:
        args.append(carry)
        in_specs.append(IN_HBM)
        aliases = {8: 0}
        kernel_fn = kernel
    return pl.pallas_call(
        kernel_fn,
        out_shape=[
            jax.ShapeDtypeStruct(state.shape, F32),
            jax.ShapeDtypeStruct((rows, channels), F32),
        ],
        in_specs=in_specs,
        out_specs=[IN_HBM, IN_VMEM],
        scratch_shapes=[pltpu.VMEM((count, height, lanes), F32)]
        + [pltpu.VMEM((rows, width), F32)] * 3
        + [pltpu.VMEM((rows // 8 * 2 * N, 8, lanes), F32)]
        + [pltpu.SemaphoreType.DMA((count,))] * 2,
        input_output_aliases=aliases,
        compiler_params=_params(16),
        name="ssm",
    )(*args)


def _swap(array, axis, size, bits):
    return lax.ppermute(array, axis, [(i, i ^ bits) for i in range(size)])


def _core(array):
    return _swap(array, "gy", 4, 1)


def _chip(array):
    return _swap(array, "gy", 4, 2)


def _gx(array, bits):
    return _swap(array, "gx", 4, bits)


def _order(array, *earlier):
    return lax.optimization_barrier((array, *earlier))[0]


def _add(*arrays):
    return functools.reduce(jnp.add, [a.astype(F32) for a in arrays])


def chunked(
    normed, in_weight, conv_weight, conv_bias, x_weight, dt_weight, dt_bias, a_log, skip,
    conv_state, ssm_state, out_weight
):
    steps, batch, depth = normed.shape
    channels = conv_bias.shape[0]
    gy = lax.axis_index("gy")
    place = jnp.stack([lax.axis_index("gx"), gy]).astype(jnp.int32)
    core = gy & 1
    flat_state = ssm_state.reshape(batch * N, channels)
    piece = batch // CHUNKS
    rows = steps * piece
    chunks = range(CHUNKS)
    cut = [slice(c * piece, (c + 1) * piece) for c in chunks]

    gathered = []
    before = None
    weight = load(in_weight, 0, place)
    for c in chunks:
        own = normed[:, cut[c], :].reshape(rows, depth)
        if before is not None:
            own = _order(own, before)
        two = _gx(own, 2)
        one = _gx(own, 1)
        relay = _order(two, weight)
        gathered.append((own, one, two, _gx(relay, 1)))
        before = relay

    arrived = {}
    after = weight
    for half in range(2):
        if half:
            weight = load(in_weight, 1, after)
        for c in chunks:
            pieces = (_order(gathered[c][0], after),) + gathered[c][1:]
            away = in_proj(place, pieces, weight, 1, after)
            near = _core(away)
            kept = in_proj(place, pieces, weight, 0, away)
            summed = _add(kept[0], near[0]).astype(BF)
            after = summed
            arrived[half, c] = _add(kept[1], near[1], _chip(summed)).astype(BF)

    conv_pieces, sums = [], []
    for c in chunks:
        inner = arrived[0, c].reshape(steps, piece, channels)
        history = jnp.concatenate([conv_state[:, cut[c], :], inner], axis=0).astype(F32)
        accum = conv_bias[None, None, :]
        for tap in range(CONV):
            accum = accum + conv_weight[tap][None, None, :] * history[tap : tap + steps]
        conv_out = jax.nn.silu(accum).astype(BF).reshape(rows, channels)
        conv_pieces.append(inner[steps - CONV + 1 :])

        proj = jnp.dot(conv_out, x_weight, preferred_element_type=F32)
        half_rows = rows // 2
        theirs = lax.dynamic_slice_in_dim(proj, (1 - core) * half_rows, half_rows, 0)
        mine = lax.dynamic_slice_in_dim(proj, core * half_rows, half_rows, 0)
        mine = _add(mine, _core(theirs.astype(BF)))
        mine = _add(mine, _chip(mine.astype(BF)))
        mine = _add(mine, _gx(mine.astype(BF), 1))
        mine = _add(mine, _gx(mine.astype(BF), 2)).astype(BF)
        sibling = _core(mine)
        both = jnp.where(
            core == 0,
            jnp.concatenate([mine, sibling], axis=0),
            jnp.concatenate([sibling, mine], axis=0),
        )
        low = both[:, :DT]
        b_c = both[:, DT:].astype(F32)

        sums.append((low, b_c, conv_out))

    scan = functools.partial(
        ssm, dt_weight=dt_weight, dt_bias=dt_bias[None, :], skip=skip[None, :], a_log=a_log,
        state=flat_state,
    )

    def gate_by(c, result):
        return (result * jax.nn.silu(arrived[1, c].astype(F32))).astype(BF)

    def finish(own, first, second):
        return _add(own, first, second).astype(BF).reshape(steps, piece, depth)

    low, b_c, conv_out = sums[0]
    carry, result = scan(0, steps, _order(low, arrived[1, 0]), b_c, conv_out, carry=None)
    gated0 = gate_by(0, result)
    across0 = _chip(gated0)
    carry, result = scan(1, steps, *sums[1], carry=carry)
    gated1 = gate_by(1, result)
    across1 = _chip(gated1)
    three0, two0, one0, own0 = out_proj(
        place, (gated0, _core(gated0), across0, _core(across0)), out_weight
    )
    three0 = _gx(three0, 1)
    one0 = _gx(one0, 1)
    across1 = _order(across1, own0)
    three1, two1, one1, own1 = out_proj(
        place, (gated1, _core(gated1), across1, _core(across1)), out_weight
    )
    three1 = _gx(_order(three1, three0, one0), 1)
    one1 = _gx(one1, 1)
    two0 = _gx(_add(two0, three0).astype(BF), 2)
    two1 = _gx(_add(two1, three1).astype(BF), 2)
    return (
        jnp.concatenate([finish(own0, one0, two0), finish(own1, one1, two1)], axis=1),
        jnp.concatenate(conv_pieces, axis=1),
        carry.reshape(ssm_state.shape),
    )


def per_device(
    normed,
    in_weight,
    conv_weight,
    conv_bias,
    x_weight,
    dt_weight,
    dt_bias,
    a_log,
    skip,
    conv_state,
    ssm_state,
    out_weight,
):
    a_rate = -jnp.exp(a_log)
    conv = conv_state
    state = ssm_state
    outputs = []
    for position in range(normed.shape[0]):
        partial_value = jnp.einsum(
            "rd,hde->rhe",
            lax.all_gather(normed[position], "gx", axis=1, tiled=True),
            in_weight,
            preferred_element_type=jnp.float32,
        )
        both_halves = lax.psum_scatter(
            partial_value.astype(jnp.bfloat16), "gy", scatter_dimension=2, tiled=True
        )
        inner_input = both_halves[:, 0, :]
        gate_input = both_halves[:, 1, :]
        accum = conv_bias[None, :] + conv_weight[CONV - 1][None, :] * inner_input.astype(
            jnp.float32
        )
        for tap in range(CONV - 1):
            accum = accum + conv_weight[tap][None, :] * conv[tap].astype(jnp.float32)
        conv_out = jax.nn.silu(accum).astype(jnp.bfloat16)
        conv = jnp.concatenate([conv[1:], inner_input[None]], axis=0)
        proj = lax.psum(
            jnp.dot(conv_out, x_weight, preferred_element_type=jnp.float32), ("gx", "gy")
        )
        step_low = proj[:, :DT].astype(jnp.bfloat16)
        b_in = proj[:, DT : DT + N]
        c_out = proj[:, DT + N :]
        delta = jax.nn.softplus(
            jnp.dot(step_low, dt_weight, preferred_element_type=jnp.float32) + dt_bias[None, :]
        )
        conv_float = conv_out.astype(jnp.float32)
        state = (
            jnp.exp(delta[:, None, :] * a_rate[None, :, :]) * state
            + delta[:, None, :] * b_in[:, :, None] * conv_float[:, None, :]
        )
        result = jnp.sum(c_out[:, :, None] * state, axis=1) + skip[None, :] * conv_float
        gated = (result * jax.nn.silu(gate_input.astype(jnp.float32))).astype(jnp.bfloat16)
        out_partial = jnp.dot(
            lax.all_gather(gated, "gy", axis=1, tiled=True),
            out_weight,
            preferred_element_type=jnp.float32,
        )
        outputs.append(
            lax.psum_scatter(
                out_partial.astype(jnp.bfloat16), "gx", scatter_dimension=1, tiled=True
            )
        )
    return (jnp.stack(outputs, axis=0), conv, state)


def solution(mesh):
    narrow = mesh.shape["gx"] == 4 and mesh.shape["gy"] == 4
    return jax.shard_map(
        chunked if narrow else per_device,
        mesh=mesh,
        in_specs=(
            P(None, "rep", ("gy", "gx")),
            P(None, "gy", "gx"),
            P(None, ("gx", "gy")),
            P(("gx", "gy")),
            P(("gx", "gy"), None),
            P(None, ("gx", "gy")),
            P(("gx", "gy")),
            P(None, ("gx", "gy")),
            P(("gx", "gy")),
            P(None, "rep", ("gx", "gy")),
            P("rep", None, ("gx", "gy")),
            P("gx", "gy"),
        ),
        out_specs=(
            P(None, "rep", ("gy", "gx")),
            P(None, "rep", ("gx", "gy")),
            P("rep", None, ("gx", "gy")),
        ),
        check_vma=False,
    )
```

```python
import functools

import jax
import jax.numpy as jnp
from jax import lax
from jax.experimental import pallas as pl
from jax.experimental.pallas import tpu as pltpu
from jax.sharding import PartitionSpec as P

N = 16
CONV = 4
DT = 512
CHUNKS = 2
LOG2E = 1.4426950408889634
BF = jnp.bfloat16
F32 = jnp.float32
IN_VMEM = pl.BlockSpec(memory_space=pltpu.VMEM)
ANYWHERE = pl.BlockSpec(memory_space=pl.ANY)
IN_HBM = pl.BlockSpec(memory_space=pltpu.HBM)
SCALARS = pl.BlockSpec(memory_space=pltpu.SMEM)


def _cost(microseconds):
    return pl.CostEstimate(
        flops=int(microseconds * 1.1e9), bytes_accessed=1, transcendentals=0
    )


def _params(mib):
    return pltpu.CompilerParams(vmem_limit_bytes=mib * 1024 * 1024)


def _load_kernel(half, source, _, target, sem):
    copy = pltpu.make_async_copy(source if half is None else source.at[half], target, sem)
    copy.start()
    copy.wait()


def load(weight, half, after):
    return pl.pallas_call(
        functools.partial(_load_kernel, half),
        out_shape=jax.ShapeDtypeStruct(weight.shape[-2:], weight.dtype),
        in_specs=[ANYWHERE] * 2,
        out_specs=IN_VMEM,
        scratch_shapes=[pltpu.SemaphoreType.DMA],
        compiler_params=_params(8),
        name="load",
    )(weight, after)


def _held_kernel(sibling, place, *refs):
    *pieces, weight, _, out = refs
    depth = pieces[0].shape[1]
    channels = out.shape[2]
    core = jnp.bitwise_xor(jnp.bitwise_and(place[1], 1), sibling)
    for i in range(2):
        chip = jnp.bitwise_xor(jnp.right_shift(place[1], 1), 1 - i)
        columns = pl.ds(pl.multiple_of((chip * 2 + core) * channels, channels), channels)
        total = None
        for k, piece in enumerate(pieces):
            start = pl.multiple_of(jnp.bitwise_xor(place[0], k) * depth, depth)
            part = jnp.dot(
                piece[...], weight[pl.ds(start, depth), columns], preferred_element_type=F32
            )
            total = part if total is None else total + part
        out[i] = total.astype(out.dtype)


def held_proj(place, pieces, weight, sibling, after):
    rows = pieces[0].shape[0]
    channels = weight.shape[1] // 4
    return pl.pallas_call(
        functools.partial(_held_kernel, sibling),
        out_shape=jax.ShapeDtypeStruct((2, rows, channels), BF),
        in_specs=[SCALARS] + [IN_VMEM] * (len(pieces) + 1) + [ANYWHERE],
        out_specs=IN_VMEM,
        cost_estimate=_cost(100),
        compiler_params=_params(8),
        name="in_proj",
    )(place, *pieces, weight, after)


def _out_kernel(place, g0, g1, g2, g3, weight, *refs):
    *outs, held, sems = refs
    channels = g0.shape[1]
    count, _, width = held.shape
    copies = []
    for i in range(count):
        target = jnp.bitwise_xor(place[0], 3 - i)
        copies.append(
            pltpu.make_async_copy(
                weight.at[:, pl.ds(pl.multiple_of(target * width, width), width)],
                held.at[i],
                sems.at[i],
            )
        )
        copies[i].start()
    for i, out in enumerate(outs):
        copies[i].wait()
        total = None
        for k, piece in enumerate((g0, g1, g2, g3)):
            start = pl.multiple_of(jnp.bitwise_xor(place[1], k) * channels, channels)
            part = jnp.dot(
                piece[...], held[i, pl.ds(start, channels), :], preferred_element_type=F32
            )
            total = part if total is None else total + part
        out[...] = total.astype(out.dtype)


def out_proj(place, pieces, out_weight):
    rows = pieces[0].shape[0]
    width = out_weight.shape[1] // 4
    return pl.pallas_call(
        _out_kernel,
        out_shape=[jax.ShapeDtypeStruct((rows, width), BF)] * 4,
        in_specs=[SCALARS] + [IN_VMEM] * 4 + [IN_HBM],
        out_specs=[IN_VMEM] * 4,
        scratch_shapes=[
            pltpu.VMEM((4, out_weight.shape[0], width), BF),
            pltpu.SemaphoreType.DMA((4,)),
        ],
        cost_estimate=_cost(0.001),
        compiler_params=_params(50),
        name="out_proj",
    )(place, *pieces, out_weight)


def _ssm_kernel(
    chunk, steps, low, bc, conv_out, dt_weight, dt_bias, skip, a_log, state, _, new_state, mixed,
    held, delta, conv, result, spread, arrive, leave
):
    batch = low.shape[0] // steps
    count, height, lanes = held.shape
    mine = pl.ds(chunk * height, height)
    columns = [pl.ds(j * lanes, lanes) for j in range(count)]
    copies = [
        pltpu.make_async_copy(state.at[mine, columns[j]], held.at[j], arrive.at[j])
        for j in range(count)
    ]
    for copy in copies:
        copy.start()

    for group in range(steps * batch // 8):
        some = bc[group * 8 : group * 8 + 8, :]
        for n in range(2 * N):
            spread[group * 2 * N + n] = jnp.broadcast_to(some[:, n : n + 1], (8, lanes))

    width = delta.shape[1]
    per = width // lanes
    outgoing = []
    for j in range(0, count, per):
        here = slice(j * lanes, j * lanes + width)
        delta[...] = jax.nn.softplus(
            jnp.dot(low[...], dt_weight[:, here], preferred_element_type=F32) + dt_bias[:, here]
        )
        conv[...] = conv_out[:, here].astype(F32)
        rate = jnp.exp(a_log[:, here]) * (-LOG2E)
        for h in range(per):
            copies[j + h].wait()

        def rows_of(block, carry, j=j, rate=rate):
            first = pl.multiple_of(block * 8, 8)
            pairs = [(t, h) for t in range(steps) for h in range(per)]
            d, dx, acc = {}, {}, {}
            for t, h in pairs:
                place = pl.ds(t * batch + first, 8), slice(h * lanes, (h + 1) * lanes)
                d[t, h] = delta[place]
                dx[t, h] = d[t, h] * conv[place]
            for n in range(N):
                rows = pl.ds(first * N + n, 8, stride=N)
                s = [held[j + h, rows, :] for h in range(per)]
                a = [
                    jnp.broadcast_to(rate[n : n + 1, h * lanes : (h + 1) * lanes], (8, lanes))
                    for h in range(per)
                ]
                for t in range(steps):
                    group = (t * (batch // 8) + block) * 2 * N
                    b = spread[group + n]
                    c = spread[group + N + n]
                    for h in range(per):
                        s[h] = jnp.exp2(d[t, h] * a[h]) * s[h] + dx[t, h] * b
                        y = c * s[h]
                        acc[t, h] = y if n == 0 else acc[t, h] + y
                for h in range(per):
                    held[j + h, rows, :] = s[h]
            for t, h in pairs:
                place = pl.ds(t * batch + first, 8), slice(h * lanes, (h + 1) * lanes)
                result[place] = acc[t, h]
            return carry

        lax.fori_loop(0, batch // 8, rows_of, 0)
        for h in range(per):
            copy = pltpu.make_async_copy(
                held.at[j + h], new_state.at[mine, columns[j + h]], leave.at[j + h]
            )
            copy.start()
            outgoing.append(copy)
        mixed[:, here] = result[...] + skip[:, here] * conv[...]
    for copy in outgoing:
        copy.wait()


def ssm(chunk, steps, low, bc, conv_out, dt_weight, dt_bias, skip, a_log, state, carry):
    rows, channels = conv_out.shape
    height = rows // steps * N
    lanes = 128
    count = channels // lanes
    width = 2 * lanes
    kernel = functools.partial(_ssm_kernel, chunk, steps)
    args = [low, bc, conv_out, dt_weight, dt_bias, skip, a_log, state]
    in_specs = [IN_VMEM] * 7 + [IN_HBM]
    aliases = {}
    if carry is None:
        kernel_fn = lambda *refs: kernel(*refs[:8], None, *refs[8:])
    else:
        args.append(carry)
        in_specs.append(IN_HBM)
        aliases = {8: 0}
        kernel_fn = kernel
    return pl.pallas_call(
        kernel_fn,
        out_shape=[
            jax.ShapeDtypeStruct(state.shape, F32),
            jax.ShapeDtypeStruct((rows, channels), F32),
        ],
        in_specs=in_specs,
        out_specs=[IN_HBM, IN_VMEM],
        scratch_shapes=[pltpu.VMEM((count, height, lanes), F32)]
        + [pltpu.VMEM((rows, width), F32)] * 3
        + [pltpu.VMEM((rows // 8 * 2 * N, 8, lanes), F32)]
        + [pltpu.SemaphoreType.DMA((count,))] * 2,
        input_output_aliases=aliases,
        cost_estimate=_cost(0.001),
        compiler_params=_params(16),
        name="ssm",
    )(*args)


def _swap(array, axis, size, bits):
    return lax.ppermute(array, axis, [(i, i ^ bits) for i in range(size)])


def _core(array):
    return _swap(array, "gy", 4, 1)


def _chip(array):
    return _swap(array, "gy", 4, 2)


def _gx(array, bits):
    return _swap(array, "gx", 4, bits)


def _order(array, *earlier):
    return lax.optimization_barrier((array, *earlier))[0]


def _add(*arrays):
    return functools.reduce(jnp.add, [a.astype(F32) for a in arrays])


def chunked(
    normed, in_weight, conv_weight, conv_bias, x_weight, dt_weight, dt_bias, a_log, skip,
    conv_state, ssm_state, out_weight
):
    steps, batch, depth = normed.shape
    channels = conv_bias.shape[0]
    gy = lax.axis_index("gy")
    place = jnp.stack([lax.axis_index("gx"), gy]).astype(jnp.int32)
    core = gy & 1
    flat_state = ssm_state.reshape(batch * N, channels)
    piece = batch // CHUNKS
    rows = steps * piece
    chunks = range(CHUNKS)
    cut = [slice(c * piece, (c + 1) * piece) for c in chunks]


    half_rows = rows // 2
    kept, near = {}, {}

    def multiply(half, c, pieces, after):
        away = held_proj(place, pieces, weights[half], 1, after)
        near[half, c] = _core(away)
        kept[half, c] = held_proj(place, pieces, weights[half], 0, away)
        return away

    def cross(c, half):
        summed = _add(kept[half, c][0], near[half, c][0]).astype(BF)
        return summed, (kept[half, c][1], near[half, c][1], _chip(summed))

    def convolve(c, parts):
        values = _add(*parts).astype(BF).reshape(steps, piece, channels)
        history = jnp.concatenate([conv_state[:, cut[c], :], values], axis=0).astype(F32)
        accum = conv_bias[None, None, :]
        for tap in range(CONV):
            accum = accum + conv_weight[tap][None, None, :] * history[tap : tap + steps]
        conv_out = jax.nn.silu(accum).astype(BF).reshape(rows, channels)
        return conv_out, values[steps - CONV + 1 :]

    def project(conv_out):
        proj = jnp.dot(conv_out, x_weight, preferred_element_type=F32)
        theirs = lax.dynamic_slice_in_dim(proj, (1 - core) * half_rows, half_rows, 0)
        mine = lax.dynamic_slice_in_dim(proj, core * half_rows, half_rows, 0)
        theirs = theirs.astype(BF)
        mine = _add(mine, _core(theirs))
        return theirs, mine, mine.astype(BF)

    one_away = lambda array: _gx(array, 1)
    two_away = lambda array: _gx(array, 2)

    def reduce(mine, sent):
        mine = _add(mine, _chip(sent))
        mine = _add(mine, one_away(mine.astype(BF)))
        mine = _add(mine, two_away(mine.astype(BF))).astype(BF)
        sibling = _core(mine)
        first = jnp.where(core == 0, mine, sibling)
        second = jnp.where(core == 0, sibling, mine)
        both = jnp.concatenate([first, second], axis=0)
        return mine, both[:, :DT], both[:, DT:].astype(F32)

    owns = [normed[:, cut[c], :].reshape(rows, depth) for c in chunks]
    weights = [load(in_weight, 0, place)]
    held0 = weights[0]
    two = _gx(owns[0], 2)
    one = _gx(owns[0], 1)
    relay = _order(two, held0)
    pieces0 = (owns[0], one, two, _gx(relay, 1))
    second = _order(owns[1], relay)
    two = _gx(second, 2)
    one = _gx(second, 1)
    away0 = multiply(0, 0, pieces0, held0)
    kept0 = kept[0, 0]
    summed0, parts = cross(0, 0)
    pieces1 = (second, one, two, _gx(_order(two, summed0), 1))
    conv0, next0 = convolve(0, parts)
    theirs0, mine, far0 = project(conv0)
    multiply(0, 1, (_order(second, summed0), *pieces1[1:]), summed0)
    summed1, parts = cross(1, 0)
    fin0, low0, b_c0 = reduce(mine, far0)
    weights.append(load(in_weight, 1, summed1))
    ag0 = multiply(1, 0, (_order(owns[0], summed1), *pieces0[1:]), weights[1])
    kg0 = kept[1, 0]
    left, right, over = parts
    conv1, next1 = convolve(1, (left, right, _order(over, kg0)))
    theirs1, mine, far1 = project(conv1)
    kept[1, 0] = _order(kept[1, 0], far1)
    sg0, gate0 = cross(0, 1)
    multiply(1, 1, (_order(second, sg0), *pieces1[1:]), kg0)
    fin1, low1, b_c1 = reduce(mine, far1)
    kept[1, 1] = _order(kept[1, 1], far1)
    gate1 = cross(1, 1)[1]
    gate0 = _add(*gate0).astype(BF)
    gate1 = _add(*gate1).astype(BF)

    scan = functools.partial(
        ssm, dt_weight=dt_weight, dt_bias=dt_bias[None, :], skip=skip[None, :], a_log=a_log,
        state=flat_state,
    )

    def gate_by(gate, result):
        return (result * jax.nn.silu(gate.astype(F32))).astype(BF)

    def finish(own, first, second):
        return _add(own, first, second).astype(BF).reshape(steps, piece, depth)

    carry, result = scan(0, steps, _order(low0, gate0), b_c0, conv0, carry=None)
    gated0 = gate_by(gate0, result)
    across0 = _chip(gated0)
    carry, result = scan(1, steps, low1, b_c1, conv1, carry=carry)
    gated1 = gate_by(gate1, result)
    across1 = _chip(gated1)
    three0, two0, one0, own0 = out_proj(
        place, (gated0, _core(gated0), across0, _core(across0)), out_weight
    )
    three0 = _gx(three0, 1)
    one0 = _gx(one0, 1)
    joined0 = _add(two0, three0).astype(BF)
    two0 = _gx(joined0, 2)
    near1 = _core(across1)
    three1, two1, one1, own1 = out_proj(
        place, (gated1, _core(gated1), across1, near1), out_weight
    )
    three1 = _gx(_order(three1, one0), 1)
    one1 = _gx(one1, 1)
    two1 = _gx(_add(two1, three1).astype(BF), 2)
    return (
        jnp.concatenate([finish(own0, one0, two0), finish(own1, one1, two1)], axis=1),
        jnp.concatenate([next0, next1], axis=1),
        carry.reshape(ssm_state.shape),
    )


def per_device(
    normed,
    in_weight,
    conv_weight,
    conv_bias,
    x_weight,
    dt_weight,
    dt_bias,
    a_log,
    skip,
    conv_state,
    ssm_state,
    out_weight,
):
    a_rate = -jnp.exp(a_log)
    conv = conv_state
    state = ssm_state
    outputs = []
    for position in range(normed.shape[0]):
        partial_value = jnp.einsum(
            "rd,hde->rhe",
            lax.all_gather(normed[position], "gx", axis=1, tiled=True),
            in_weight,
            preferred_element_type=jnp.float32,
        )
        both_halves = lax.psum_scatter(
            partial_value.astype(jnp.bfloat16), "gy", scatter_dimension=2, tiled=True
        )
        inner_input = both_halves[:, 0, :]
        gate_input = both_halves[:, 1, :]
        accum = conv_bias[None, :] + conv_weight[CONV - 1][None, :] * inner_input.astype(
            jnp.float32
        )
        for tap in range(CONV - 1):
            accum = accum + conv_weight[tap][None, :] * conv[tap].astype(jnp.float32)
        conv_out = jax.nn.silu(accum).astype(jnp.bfloat16)
        conv = jnp.concatenate([conv[1:], inner_input[None]], axis=0)
        proj = lax.psum(
            jnp.dot(conv_out, x_weight, preferred_element_type=jnp.float32), ("gx", "gy")
        )
        step_low = proj[:, :DT].astype(jnp.bfloat16)
        b_in = proj[:, DT : DT + N]
        c_out = proj[:, DT + N :]
        delta = jax.nn.softplus(
            jnp.dot(step_low, dt_weight, preferred_element_type=jnp.float32) + dt_bias[None, :]
        )
        conv_float = conv_out.astype(jnp.float32)
        state = (
            jnp.exp(delta[:, None, :] * a_rate[None, :, :]) * state
            + delta[:, None, :] * b_in[:, :, None] * conv_float[:, None, :]
        )
        result = jnp.sum(c_out[:, :, None] * state, axis=1) + skip[None, :] * conv_float
        gated = (result * jax.nn.silu(gate_input.astype(jnp.float32))).astype(jnp.bfloat16)
        out_partial = jnp.dot(
            lax.all_gather(gated, "gy", axis=1, tiled=True),
            out_weight,
            preferred_element_type=jnp.float32,
        )
        outputs.append(
            lax.psum_scatter(
                out_partial.astype(jnp.bfloat16), "gx", scatter_dimension=1, tiled=True
            )
        )
    return (jnp.stack(outputs, axis=0), conv, state)


def solution(mesh):
    narrow = mesh.shape["gx"] == 4 and mesh.shape["gy"] == 4
    return jax.shard_map(
        chunked if narrow else per_device,
        mesh=mesh,
        in_specs=(
            P(None, "rep", ("gy", "gx")),
            P(None, "gy", "gx"),
            P(None, ("gx", "gy")),
            P(("gx", "gy")),
            P(("gx", "gy"), None),
            P(None, ("gx", "gy")),
            P(("gx", "gy")),
            P(None, ("gx", "gy")),
            P(("gx", "gy")),
            P(None, "rep", ("gx", "gy")),
            P("rep", None, ("gx", "gy")),
            P("gx", "gy"),
        ),
        out_specs=(
            P(None, "rep", ("gy", "gx")),
            P(None, "rep", ("gx", "gy")),
            P("rep", None, ("gx", "gy")),
        ),
        check_vma=False,
    )
```

```python
import functools

import jax
import jax.numpy as jnp
from jax import lax
from jax.experimental import pallas as pl
from jax.experimental.pallas import tpu as pltpu
from jax.sharding import PartitionSpec as P

N = 16
CONV = 4
DT = 512
CHUNKS = 2
LOG2E = 1.4426950408889634
BF = jnp.bfloat16
F32 = jnp.float32
IN_VMEM = pl.BlockSpec(memory_space=pltpu.VMEM)
ANYWHERE = pl.BlockSpec(memory_space=pl.ANY)
IN_HBM = pl.BlockSpec(memory_space=pltpu.HBM)
SCALARS = pl.BlockSpec(memory_space=pltpu.SMEM)


def _cost(microseconds):
    return pl.CostEstimate(
        flops=int(microseconds * 1.1e9), bytes_accessed=1, transcendentals=0
    )


def _params(mib):
    return pltpu.CompilerParams(vmem_limit_bytes=mib * 1024 * 1024)


def _in_kernel(half, cores, place, *refs):
    *refs, held, sems = refs
    outs = refs[-len(cores) :]
    *pieces, weight, _ = refs[: -len(cores)]
    depth = pieces[0].shape[1]
    channels = outs[0].shape[2]
    width = held.shape[2]
    tiles = []
    for out, sibling in zip(outs, cores):
        core = jnp.bitwise_xor(jnp.bitwise_and(place[1], 1), sibling)
        for i in range(2):
            chip = jnp.bitwise_xor(jnp.right_shift(place[1], 1), 1 - i)
            for column in range(0, channels, width):
                first = pl.multiple_of((chip * 2 + core) * channels + column, width)
                slot = len(tiles)
                copy = pltpu.make_async_copy(
                    weight.at[half, :, pl.ds(first, width)], held.at[slot], sems.at[slot]
                )
                copy.start()
                tiles.append((copy, out, i, column))
    for slot, (copy, out, i, column) in enumerate(tiles):
        copy.wait()
        total = None
        for k, piece in enumerate(pieces):
            rows = pl.ds(pl.multiple_of(jnp.bitwise_xor(place[0], k) * depth, depth), depth)
            part = jnp.dot(piece[...], held[slot, rows, :], preferred_element_type=F32)
            total = part if total is None else total + part
        out[i, :, column : column + width] = total.astype(out.dtype)


def in_proj(place, pieces, weight, half, cores, after, width=512):
    rows = pieces[0].shape[0]
    channels = weight.shape[2] // 4
    count = len(cores) * 2 * channels // width
    return pl.pallas_call(
        functools.partial(_in_kernel, half, cores),
        out_shape=[jax.ShapeDtypeStruct((2, rows, channels), BF)] * len(cores),
        in_specs=[SCALARS] + [IN_VMEM] * len(pieces) + [IN_HBM, ANYWHERE],
        out_specs=[IN_VMEM] * len(cores),
        scratch_shapes=[
            pltpu.VMEM((count, weight.shape[1], width), BF),
            pltpu.SemaphoreType.DMA((count,)),
        ],
        cost_estimate=_cost(100),
        compiler_params=_params(44),
        name="in_proj",
    )(place, *pieces, weight, after)


def _out_kernel(place, g0, g1, g2, g3, weight, *refs):
    *outs, held, sems = refs
    channels = g0.shape[1]
    count, _, width = held.shape
    copies = []
    for i in range(count):
        target = jnp.bitwise_xor(place[0], 3 - i)
        copies.append(
            pltpu.make_async_copy(
                weight.at[:, pl.ds(pl.multiple_of(target * width, width), width)],
                held.at[i],
                sems.at[i],
            )
        )
        copies[i].start()
    for i, out in enumerate(outs):
        copies[i].wait()
        total = None
        for k, piece in enumerate((g0, g1, g2, g3)):
            start = pl.multiple_of(jnp.bitwise_xor(place[1], k) * channels, channels)
            part = jnp.dot(
                piece[...], held[i, pl.ds(start, channels), :], preferred_element_type=F32
            )
            total = part if total is None else total + part
        out[...] = total.astype(out.dtype)


def out_proj(place, pieces, out_weight):
    rows = pieces[0].shape[0]
    width = out_weight.shape[1] // 4
    return pl.pallas_call(
        _out_kernel,
        out_shape=[jax.ShapeDtypeStruct((rows, width), BF)] * 4,
        in_specs=[SCALARS] + [IN_VMEM] * 4 + [IN_HBM],
        out_specs=[IN_VMEM] * 4,
        scratch_shapes=[
            pltpu.VMEM((4, out_weight.shape[0], width), BF),
            pltpu.SemaphoreType.DMA((4,)),
        ],
        cost_estimate=_cost(0.001),
        compiler_params=_params(50),
        name="out_proj",
    )(place, *pieces, out_weight)


def _ssm_kernel(
    chunk, steps, low, bc, conv_out, dt_weight, dt_bias, skip, a_log, state, _, new_state, mixed,
    held, delta, conv, result, spread, arrive, leave
):
    batch = low.shape[0] // steps
    count, height, lanes = held.shape
    mine = pl.ds(chunk * height, height)
    columns = [pl.ds(j * lanes, lanes) for j in range(count)]
    copies = [
        pltpu.make_async_copy(state.at[mine, columns[j]], held.at[j], arrive.at[j])
        for j in range(count)
    ]
    for copy in copies:
        copy.start()

    for group in range(steps * batch // 8):
        some = bc[group * 8 : group * 8 + 8, :]
        for n in range(2 * N):
            spread[group * 2 * N + n] = jnp.broadcast_to(some[:, n : n + 1], (8, lanes))

    width = delta.shape[1]
    per = width // lanes
    outgoing = []
    for j in range(0, count, per):
        here = slice(j * lanes, j * lanes + width)
        delta[...] = jax.nn.softplus(
            jnp.dot(low[...], dt_weight[:, here], preferred_element_type=F32) + dt_bias[:, here]
        )
        conv[...] = conv_out[:, here].astype(F32)
        rate = jnp.exp(a_log[:, here]) * (-LOG2E)
        for h in range(per):
            copies[j + h].wait()

        def rows_of(block, carry, j=j, rate=rate):
            first = pl.multiple_of(block * 8, 8)
            pairs = [(t, h) for t in range(steps) for h in range(per)]
            d, dx, acc = {}, {}, {}
            for t, h in pairs:
                place = pl.ds(t * batch + first, 8), slice(h * lanes, (h + 1) * lanes)
                d[t, h] = delta[place]
                dx[t, h] = d[t, h] * conv[place]
            for n in range(N):
                rows = pl.ds(first * N + n, 8, stride=N)
                s = [held[j + h, rows, :] for h in range(per)]
                a = [
                    jnp.broadcast_to(rate[n : n + 1, h * lanes : (h + 1) * lanes], (8, lanes))
                    for h in range(per)
                ]
                for t in range(steps):
                    group = (t * (batch // 8) + block) * 2 * N
                    b = spread[group + n]
                    c = spread[group + N + n]
                    for h in range(per):
                        s[h] = jnp.exp2(d[t, h] * a[h]) * s[h] + dx[t, h] * b
                        y = c * s[h]
                        acc[t, h] = y if n == 0 else acc[t, h] + y
                for h in range(per):
                    held[j + h, rows, :] = s[h]
            for t, h in pairs:
                place = pl.ds(t * batch + first, 8), slice(h * lanes, (h + 1) * lanes)
                result[place] = acc[t, h]
            return carry

        lax.fori_loop(0, batch // 8, rows_of, 0)
        for h in range(per):
            copy = pltpu.make_async_copy(
                held.at[j + h], new_state.at[mine, columns[j + h]], leave.at[j + h]
            )
            copy.start()
            outgoing.append(copy)
        mixed[:, here] = result[...] + skip[:, here] * conv[...]
    for copy in outgoing:
        copy.wait()


def ssm(chunk, steps, low, bc, conv_out, dt_weight, dt_bias, skip, a_log, state, carry):
    rows, channels = conv_out.shape
    height = rows // steps * N
    lanes = 128
    count = channels // lanes
    width = 2 * lanes
    kernel = functools.partial(_ssm_kernel, chunk, steps)
    args = [low, bc, conv_out, dt_weight, dt_bias, skip, a_log, state]
    in_specs = [IN_VMEM] * 7 + [IN_HBM]
    aliases = {}
    if carry is None:
        kernel_fn = lambda *refs: kernel(*refs[:8], None, *refs[8:])
    else:
        args.append(carry)
        in_specs.append(IN_HBM)
        aliases = {8: 0}
        kernel_fn = kernel
    return pl.pallas_call(
        kernel_fn,
        out_shape=[
            jax.ShapeDtypeStruct(state.shape, F32),
            jax.ShapeDtypeStruct((rows, channels), F32),
        ],
        in_specs=in_specs,
        out_specs=[IN_HBM, IN_VMEM],
        scratch_shapes=[pltpu.VMEM((count, height, lanes), F32)]
        + [pltpu.VMEM((rows, width), F32)] * 3
        + [pltpu.VMEM((rows // 8 * 2 * N, 8, lanes), F32)]
        + [pltpu.SemaphoreType.DMA((count,))] * 2,
        input_output_aliases=aliases,
        cost_estimate=_cost(0.001),
        compiler_params=_params(16),
        name="ssm",
    )(*args)


def _swap(array, axis, size, bits):
    return lax.ppermute(array, axis, [(i, i ^ bits) for i in range(size)])


def _core(array):
    return _swap(array, "gy", 4, 1)


def _chip(array):
    return _swap(array, "gy", 4, 2)


def _gx(array, bits):
    return _swap(array, "gx", 4, bits)


def _order(array, *earlier):
    return lax.optimization_barrier((array, *earlier))[0]


def _add(*arrays):
    return functools.reduce(jnp.add, [a.astype(F32) for a in arrays])


def chunked(
    normed, in_weight, conv_weight, conv_bias, x_weight, dt_weight, dt_bias, a_log, skip,
    conv_state, ssm_state, out_weight
):
    steps, batch, depth = normed.shape
    channels = conv_bias.shape[0]
    gy = lax.axis_index("gy")
    place = jnp.stack([lax.axis_index("gx"), gy]).astype(jnp.int32)
    core = gy & 1
    flat_state = ssm_state.reshape(batch * N, channels)
    piece = batch // CHUNKS
    rows = steps * piece
    chunks = range(CHUNKS)
    cut = [slice(c * piece, (c + 1) * piece) for c in chunks]


    half_rows = rows // 2
    kept, near = {}, {}

    def multiply(half, c, pieces, after):
        if half in (0,):
            (away,) = in_proj(place, pieces, in_weight, half, (1,), after)
            near[half, c] = _core(away)
            (kept[half, c],) = in_proj(place, pieces, in_weight, half, (0,), away)
        else:
            away, kept[half, c] = in_proj(place, pieces, in_weight, half, (1, 0), after)
            near[half, c] = _core(away)
        return away

    def cross(c, half):
        summed = _add(kept[half, c][0], near[half, c][0]).astype(BF)
        return summed, (kept[half, c][1], near[half, c][1], _chip(summed))

    def convolve(c, parts):
        values = _add(*parts).astype(BF).reshape(steps, piece, channels)
        history = jnp.concatenate([conv_state[:, cut[c], :], values], axis=0).astype(F32)
        accum = conv_bias[None, None, :]
        for tap in range(CONV):
            accum = accum + conv_weight[tap][None, None, :] * history[tap : tap + steps]
        conv_out = jax.nn.silu(accum).astype(BF).reshape(rows, channels)
        return conv_out, values[steps - CONV + 1 :]

    def project(conv_out):
        proj = jnp.dot(conv_out, x_weight, preferred_element_type=F32)
        theirs = lax.dynamic_slice_in_dim(proj, (1 - core) * half_rows, half_rows, 0)
        mine = lax.dynamic_slice_in_dim(proj, core * half_rows, half_rows, 0)
        theirs = theirs.astype(BF)
        mine = _add(mine, _core(theirs))
        return theirs, mine, mine.astype(BF)

    one_away = lambda array: _gx(array, 1)
    two_away = lambda array: _gx(array, 2)

    def reduce(mine, sent):
        mine = _add(mine, _chip(sent))
        mine = _add(mine, one_away(mine.astype(BF)))
        mine = _add(mine, two_away(mine.astype(BF))).astype(BF)
        sibling = _core(mine)
        first = jnp.where(core == 0, mine, sibling)
        second = jnp.where(core == 0, sibling, mine)
        both = jnp.concatenate([first, second], axis=0)
        return mine, both[:, :DT], both[:, DT:].astype(F32)

    owns = [normed[:, cut[c], :].reshape(rows, depth) for c in chunks]
    held0 = place
    two = _gx(owns[0], 2)
    one = _gx(owns[0], 1)
    relay = two
    pieces0 = (owns[0], one, two, _gx(relay, 1))
    second = _order(owns[1], relay)
    two = _gx(second, 2)
    one = _gx(second, 1)
    away0 = multiply(0, 0, pieces0, held0)
    kept0 = kept[0, 0]
    summed0, parts = cross(0, 0)
    pieces1 = (second, one, two, _gx(_order(two, summed0), 1))
    conv0, next0 = convolve(0, parts)
    theirs0, mine, far0 = project(conv0)
    multiply(0, 1, (_order(second, summed0), *pieces1[1:]), summed0)
    summed1, parts = cross(1, 0)
    fin0, low0, b_c0 = reduce(mine, far0)
    ag0 = multiply(1, 0, (_order(owns[0], summed1), *pieces0[1:]), summed1)
    kg0 = kept[1, 0]
    left, right, over = parts
    conv1, next1 = convolve(1, (left, right, _order(over, kg0)))
    theirs1, mine, far1 = project(conv1)
    kept[1, 0] = _order(kept[1, 0], far1)
    sg0, gate0 = cross(0, 1)
    multiply(1, 1, (_order(second, sg0), *pieces1[1:]), kg0)
    fin1, low1, b_c1 = reduce(mine, far1)
    kept[1, 1] = _order(kept[1, 1], far1)
    gate1 = cross(1, 1)[1]
    gate0 = _add(*gate0).astype(BF)
    gate1 = _add(*gate1).astype(BF)

    scan = functools.partial(
        ssm, dt_weight=dt_weight, dt_bias=dt_bias[None, :], skip=skip[None, :], a_log=a_log,
        state=flat_state,
    )

    def gate_by(gate, result):
        return (result * jax.nn.silu(gate.astype(F32))).astype(BF)

    def finish(own, first, second):
        return _add(own, first, second).astype(BF).reshape(steps, piece, depth)

    carry, result = scan(0, steps, _order(low0, gate0), b_c0, conv0, carry=None)
    gated0 = gate_by(gate0, result)
    across0 = _chip(gated0)
    carry, result = scan(1, steps, low1, b_c1, conv1, carry=carry)
    gated1 = gate_by(gate1, result)
    across1 = _chip(gated1)
    three0, two0, one0, own0 = out_proj(
        place, (gated0, _core(gated0), across0, _core(across0)), out_weight
    )
    three0 = _gx(three0, 1)
    one0 = _gx(one0, 1)
    joined0 = _add(two0, three0).astype(BF)
    two0 = _gx(joined0, 2)
    near1 = _core(across1)
    three1, two1, one1, own1 = out_proj(
        place, (gated1, _core(gated1), across1, near1), out_weight
    )
    three1 = _gx(_order(three1, one0), 1)
    one1 = _gx(one1, 1)
    two1 = _gx(_add(two1, three1).astype(BF), 2)
    return (
        jnp.concatenate([finish(own0, one0, two0), finish(own1, one1, two1)], axis=1),
        jnp.concatenate([next0, next1], axis=1),
        carry.reshape(ssm_state.shape),
    )


def per_device(
    normed,
    in_weight,
    conv_weight,
    conv_bias,
    x_weight,
    dt_weight,
    dt_bias,
    a_log,
    skip,
    conv_state,
    ssm_state,
    out_weight,
):
    a_rate = -jnp.exp(a_log)
    conv = conv_state
    state = ssm_state
    outputs = []
    for position in range(normed.shape[0]):
        partial_value = jnp.einsum(
            "rd,hde->rhe",
            lax.all_gather(normed[position], "gx", axis=1, tiled=True),
            in_weight,
            preferred_element_type=jnp.float32,
        )
        both_halves = lax.psum_scatter(
            partial_value.astype(jnp.bfloat16), "gy", scatter_dimension=2, tiled=True
        )
        inner_input = both_halves[:, 0, :]
        gate_input = both_halves[:, 1, :]
        accum = conv_bias[None, :] + conv_weight[CONV - 1][None, :] * inner_input.astype(
            jnp.float32
        )
        for tap in range(CONV - 1):
            accum = accum + conv_weight[tap][None, :] * conv[tap].astype(jnp.float32)
        conv_out = jax.nn.silu(accum).astype(jnp.bfloat16)
        conv = jnp.concatenate([conv[1:], inner_input[None]], axis=0)
        proj = lax.psum(
            jnp.dot(conv_out, x_weight, preferred_element_type=jnp.float32), ("gx", "gy")
        )
        step_low = proj[:, :DT].astype(jnp.bfloat16)
        b_in = proj[:, DT : DT + N]
        c_out = proj[:, DT + N :]
        delta = jax.nn.softplus(
            jnp.dot(step_low, dt_weight, preferred_element_type=jnp.float32) + dt_bias[None, :]
        )
        conv_float = conv_out.astype(jnp.float32)
        state = (
            jnp.exp(delta[:, None, :] * a_rate[None, :, :]) * state
            + delta[:, None, :] * b_in[:, :, None] * conv_float[:, None, :]
        )
        result = jnp.sum(c_out[:, :, None] * state, axis=1) + skip[None, :] * conv_float
        gated = (result * jax.nn.silu(gate_input.astype(jnp.float32))).astype(jnp.bfloat16)
        out_partial = jnp.dot(
            lax.all_gather(gated, "gy", axis=1, tiled=True),
            out_weight,
            preferred_element_type=jnp.float32,
        )
        outputs.append(
            lax.psum_scatter(
                out_partial.astype(jnp.bfloat16), "gx", scatter_dimension=1, tiled=True
            )
        )
    return (jnp.stack(outputs, axis=0), conv, state)


def solution(mesh):
    narrow = mesh.shape["gx"] == 4 and mesh.shape["gy"] == 4
    return jax.shard_map(
        chunked if narrow else per_device,
        mesh=mesh,
        in_specs=(
            P(None, "rep", ("gy", "gx")),
            P(None, "gy", "gx"),
            P(None, ("gx", "gy")),
            P(("gx", "gy")),
            P(("gx", "gy"), None),
            P(None, ("gx", "gy")),
            P(("gx", "gy")),
            P(None, ("gx", "gy")),
            P(("gx", "gy")),
            P(None, "rep", ("gx", "gy")),
            P("rep", None, ("gx", "gy")),
            P("gx", "gy"),
        ),
        out_specs=(
            P(None, "rep", ("gy", "gx")),
            P(None, "rep", ("gx", "gy")),
            P("rep", None, ("gx", "gy")),
        ),
        check_vma=False,
    )
```

```python
import functools

import jax
import jax.numpy as jnp
from jax import lax
from jax.experimental import pallas as pl
from jax.experimental.pallas import tpu as pltpu
from jax.sharding import PartitionSpec as P

N = 16
CONV = 4
DT = 512
CHUNKS = 2
LOG2E = 1.4426950408889634
BF = jnp.bfloat16
F32 = jnp.float32
IN_VMEM = pl.BlockSpec(memory_space=pltpu.VMEM)
ANYWHERE = pl.BlockSpec(memory_space=pl.ANY)
IN_HBM = pl.BlockSpec(memory_space=pltpu.HBM)
SCALARS = pl.BlockSpec(memory_space=pltpu.SMEM)


def _cost(microseconds):
    return pl.CostEstimate(
        flops=int(microseconds * 1.1e9), bytes_accessed=1, transcendentals=0
    )


def _params(mib):
    return pltpu.CompilerParams(vmem_limit_bytes=mib * 1024 * 1024)


def _in_kernel(half, cores, place, *refs):
    *refs, held, sems = refs
    outs = refs[-len(cores) :]
    *pieces, weight, _ = refs[: -len(cores)]
    depth = pieces[0].shape[1]
    channels = outs[0].shape[2]
    width = held.shape[2]
    tiles = []
    for out, sibling in zip(outs, cores):
        core = jnp.bitwise_xor(jnp.bitwise_and(place[1], 1), sibling)
        for i in range(2):
            chip = jnp.bitwise_xor(jnp.right_shift(place[1], 1), 1 - i)
            for column in range(0, channels, width):
                first = pl.multiple_of((chip * 2 + core) * channels + column, width)
                slot = len(tiles)
                copy = pltpu.make_async_copy(
                    weight.at[half, :, pl.ds(first, width)], held.at[slot], sems.at[slot]
                )
                copy.start()
                tiles.append((copy, out, i, column))
    for slot, (copy, out, i, column) in enumerate(tiles):
        copy.wait()
        total = None
        for k, piece in enumerate(pieces):
            rows = pl.ds(pl.multiple_of(jnp.bitwise_xor(place[0], k) * depth, depth), depth)
            part = jnp.dot(piece[...], held[slot, rows, :], preferred_element_type=F32)
            total = part if total is None else total + part
        out[i, :, column : column + width] = total.astype(out.dtype)


def in_proj(place, pieces, weight, half, cores, after, width=512):
    rows = pieces[0].shape[0]
    channels = weight.shape[2] // 4
    count = len(cores) * 2 * channels // width
    return pl.pallas_call(
        functools.partial(_in_kernel, half, cores),
        out_shape=[jax.ShapeDtypeStruct((2, rows, channels), BF)] * len(cores),
        in_specs=[SCALARS] + [IN_VMEM] * len(pieces) + [IN_HBM, ANYWHERE],
        out_specs=[IN_VMEM] * len(cores),
        scratch_shapes=[
            pltpu.VMEM((count, weight.shape[1], width), BF),
            pltpu.SemaphoreType.DMA((count,)),
        ],
        cost_estimate=_cost(100),
        compiler_params=_params(44),
        name="in_proj",
    )(place, *pieces, weight, after)


def _out_kernel(place, g0, g1, g2, g3, weight, *refs):
    *outs, held, sems = refs
    channels = g0.shape[1]
    count, _, width = held.shape
    copies = []
    for i in range(count):
        target = jnp.bitwise_xor(place[0], 3 - i)
        copies.append(
            pltpu.make_async_copy(
                weight.at[:, pl.ds(pl.multiple_of(target * width, width), width)],
                held.at[i],
                sems.at[i],
            )
        )
        copies[i].start()
    for i, out in enumerate(outs):
        copies[i].wait()
        total = None
        for k, piece in enumerate((g0, g1, g2, g3)):
            start = pl.multiple_of(jnp.bitwise_xor(place[1], k) * channels, channels)
            part = jnp.dot(
                piece[...], held[i, pl.ds(start, channels), :], preferred_element_type=F32
            )
            total = part if total is None else total + part
        out[...] = total.astype(out.dtype)


def out_proj(place, pieces, out_weight):
    rows = pieces[0].shape[0]
    width = out_weight.shape[1] // 4
    return pl.pallas_call(
        _out_kernel,
        out_shape=[jax.ShapeDtypeStruct((rows, width), BF)] * 4,
        in_specs=[SCALARS] + [IN_VMEM] * 4 + [IN_HBM],
        out_specs=[IN_VMEM] * 4,
        scratch_shapes=[
            pltpu.VMEM((4, out_weight.shape[0], width), BF),
            pltpu.SemaphoreType.DMA((4,)),
        ],
        cost_estimate=_cost(0.001),
        compiler_params=_params(50),
        name="out_proj",
    )(place, *pieces, out_weight)


def _ssm_kernel(
    chunk, steps, low, bc, conv_out, dt_weight, dt_bias, skip, a_log, state, _, new_state, mixed,
    held, delta, conv, result, spread, arrive, leave
):
    batch = low.shape[0] // steps
    count, height, lanes = held.shape
    mine = pl.ds(chunk * height, height)
    columns = [pl.ds(j * lanes, lanes) for j in range(count)]
    copies = [
        pltpu.make_async_copy(state.at[mine, columns[j]], held.at[j], arrive.at[j])
        for j in range(count)
    ]
    for copy in copies:
        copy.start()

    for group in range(steps * batch // 8):
        some = bc[group * 8 : group * 8 + 8, :]
        for n in range(2 * N):
            spread[group * 2 * N + n] = jnp.broadcast_to(some[:, n : n + 1], (8, lanes))

    width = delta.shape[1]
    per = width // lanes
    outgoing = []
    for j in range(0, count, per):
        here = slice(j * lanes, j * lanes + width)
        delta[...] = jax.nn.softplus(
            jnp.dot(low[...], dt_weight[:, here], preferred_element_type=F32) + dt_bias[:, here]
        )
        conv[...] = conv_out[:, here].astype(F32)
        rate = jnp.exp(a_log[:, here]) * (-LOG2E)
        for h in range(per):
            copies[j + h].wait()

        def rows_of(block, carry, j=j, rate=rate):
            first = pl.multiple_of(block * 8, 8)
            pairs = [(t, h) for t in range(steps) for h in range(per)]
            d, dx, acc = {}, {}, {}
            for t, h in pairs:
                place = pl.ds(t * batch + first, 8), slice(h * lanes, (h + 1) * lanes)
                d[t, h] = delta[place]
                dx[t, h] = d[t, h] * conv[place]
            for n in range(N):
                rows = pl.ds(first * N + n, 8, stride=N)
                s = [held[j + h, rows, :] for h in range(per)]
                a = [
                    jnp.broadcast_to(rate[n : n + 1, h * lanes : (h + 1) * lanes], (8, lanes))
                    for h in range(per)
                ]
                for t in range(steps):
                    group = (t * (batch // 8) + block) * 2 * N
                    b = spread[group + n]
                    c = spread[group + N + n]
                    for h in range(per):
                        s[h] = jnp.exp2(d[t, h] * a[h]) * s[h] + dx[t, h] * b
                        y = c * s[h]
                        acc[t, h] = y if n == 0 else acc[t, h] + y
                for h in range(per):
                    held[j + h, rows, :] = s[h]
            for t, h in pairs:
                place = pl.ds(t * batch + first, 8), slice(h * lanes, (h + 1) * lanes)
                result[place] = acc[t, h]
            return carry

        lax.fori_loop(0, batch // 8, rows_of, 0)
        for h in range(per):
            copy = pltpu.make_async_copy(
                held.at[j + h], new_state.at[mine, columns[j + h]], leave.at[j + h]
            )
            copy.start()
            outgoing.append(copy)
        mixed[:, here] = result[...] + skip[:, here] * conv[...]
    for copy in outgoing:
        copy.wait()


def ssm(chunk, steps, low, bc, conv_out, dt_weight, dt_bias, skip, a_log, state, carry):
    rows, channels = conv_out.shape
    height = rows // steps * N
    lanes = 128
    count = channels // lanes
    width = 2 * lanes
    kernel = functools.partial(_ssm_kernel, chunk, steps)
    args = [low, bc, conv_out, dt_weight, dt_bias, skip, a_log, state]
    in_specs = [IN_VMEM] * 7 + [IN_HBM]
    aliases = {}
    if carry is None:
        kernel_fn = lambda *refs: kernel(*refs[:8], None, *refs[8:])
    else:
        args.append(carry)
        in_specs.append(IN_HBM)
        aliases = {8: 0}
        kernel_fn = kernel
    return pl.pallas_call(
        kernel_fn,
        out_shape=[
            jax.ShapeDtypeStruct(state.shape, F32),
            jax.ShapeDtypeStruct((rows, channels), F32),
        ],
        in_specs=in_specs,
        out_specs=[IN_HBM, IN_VMEM],
        scratch_shapes=[pltpu.VMEM((count, height, lanes), F32)]
        + [pltpu.VMEM((rows, width), F32)] * 3
        + [pltpu.VMEM((rows // 8 * 2 * N, 8, lanes), F32)]
        + [pltpu.SemaphoreType.DMA((count,))] * 2,
        input_output_aliases=aliases,
        cost_estimate=_cost(0.001),
        compiler_params=_params(16),
        name="ssm",
    )(*args)


def _swap(array, axis, size, bits):
    return lax.ppermute(array, axis, [(i, i ^ bits) for i in range(size)])


def _core(array):
    return _swap(array, "gy", 4, 1)


def _chip(array):
    return _swap(array, "gy", 4, 2)


def _gx(array, bits):
    return _swap(array, "gx", 4, bits)


def _order(array, *earlier):
    return lax.optimization_barrier((array, *earlier))[0]


def _add(*arrays):
    return functools.reduce(jnp.add, [a.astype(F32) for a in arrays])


def chunked(
    normed, in_weight, conv_weight, conv_bias, x_weight, dt_weight, dt_bias, a_log, skip,
    conv_state, ssm_state, out_weight
):
    steps, batch, depth = normed.shape
    channels = conv_bias.shape[0]
    gy = lax.axis_index("gy")
    place = jnp.stack([lax.axis_index("gx"), gy]).astype(jnp.int32)
    core = gy & 1
    flat_state = ssm_state.reshape(batch * N, channels)
    piece = batch // CHUNKS
    rows = steps * piece
    chunks = range(CHUNKS)
    cut = [slice(c * piece, (c + 1) * piece) for c in chunks]


    half_rows = rows // 2
    kept, near = {}, {}

    def multiply(half, c, pieces, after):
        if half in (0,):
            (away,) = in_proj(place, pieces, in_weight, half, (1,), after)
            near[half, c] = _core(away)
            (kept[half, c],) = in_proj(place, pieces, in_weight, half, (0,), away)
        else:
            away, kept[half, c] = in_proj(place, pieces, in_weight, half, (1, 0), after)
            near[half, c] = _core(away)
        return away

    def cross(c, half):
        summed = _add(kept[half, c][0], near[half, c][0]).astype(BF)
        return summed, (kept[half, c][1], near[half, c][1], _chip(summed))

    def convolve(c, parts):
        values = _add(*parts).astype(BF).reshape(steps, piece, channels)
        history = jnp.concatenate([conv_state[:, cut[c], :], values], axis=0).astype(F32)
        accum = conv_bias[None, None, :]
        for tap in range(CONV):
            accum = accum + conv_weight[tap][None, None, :] * history[tap : tap + steps]
        conv_out = jax.nn.silu(accum).astype(BF).reshape(rows, channels)
        return conv_out, values[steps - CONV + 1 :]

    def project(conv_out):
        proj = jnp.dot(conv_out, x_weight, preferred_element_type=F32)
        theirs = lax.dynamic_slice_in_dim(proj, (1 - core) * half_rows, half_rows, 0)
        mine = lax.dynamic_slice_in_dim(proj, core * half_rows, half_rows, 0)
        theirs = theirs.astype(BF)
        mine = _add(mine, _core(theirs))
        return theirs, mine, mine.astype(BF)

    one_away = lambda array: _gx(array, 1)
    two_away = lambda array: _gx(array, 2)

    def reduce(mine, sent):
        mine = _add(mine, _chip(sent))
        mine = _add(mine, one_away(mine.astype(BF)))
        mine = _add(mine, two_away(mine.astype(BF))).astype(BF)
        sibling = _core(mine)
        first = jnp.where(core == 0, mine, sibling)
        second = jnp.where(core == 0, sibling, mine)
        both = jnp.concatenate([first, second], axis=0)
        return mine, both[:, :DT], both[:, DT:].astype(F32)

    owns = [normed[:, cut[c], :].reshape(rows, depth) for c in chunks]
    held0 = place
    two = _gx(owns[0], 2)
    one = _gx(owns[0], 1)
    relay = two
    pieces0 = (owns[0], one, two, _gx(relay, 1))
    second = _order(owns[1], relay)
    two = _gx(second, 2)
    one = _gx(second, 1)
    away0 = multiply(0, 0, pieces0, held0)
    kept0 = kept[0, 0]
    summed0, parts = cross(0, 0)
    pieces1 = (second, one, two, _gx(_order(two, kept0), 1))
    conv0, next0 = convolve(0, parts)
    theirs0, mine, far0 = project(conv0)
    multiply(0, 1, (_order(second, summed0), *pieces1[1:]), summed0)
    summed1, parts = cross(1, 0)
    fin0, low0, b_c0 = reduce(mine, far0)
    ag0 = multiply(1, 0, (_order(owns[0], summed1), *pieces0[1:]), summed1)
    kg0 = kept[1, 0]
    left, right, over = parts
    conv1, next1 = convolve(1, (left, right, _order(over, kg0)))
    theirs1, mine, far1 = project(conv1)
    kept[1, 0] = _order(kept[1, 0], far1)
    sg0, gate0 = cross(0, 1)
    multiply(1, 1, (_order(second, sg0), *pieces1[1:]), kg0)
    fin1, low1, b_c1 = reduce(mine, far1)
    kept[1, 1] = _order(kept[1, 1], far1)
    gate1 = cross(1, 1)[1]
    gate0 = _add(*gate0).astype(BF)
    gate1 = _add(*gate1).astype(BF)

    scan = functools.partial(
        ssm, dt_weight=dt_weight, dt_bias=dt_bias[None, :], skip=skip[None, :], a_log=a_log,
        state=flat_state,
    )

    def gate_by(gate, result):
        return (result * jax.nn.silu(gate.astype(F32))).astype(BF)

    def finish(own, first, second):
        return _add(own, first, second).astype(BF).reshape(steps, piece, depth)

    carry, result = scan(0, steps, _order(low0, gate0), b_c0, conv0, carry=None)
    gated0 = gate_by(gate0, result)
    across0 = _chip(gated0)
    carry, result = scan(1, steps, low1, b_c1, conv1, carry=carry)
    gated1 = gate_by(gate1, result)
    across1 = _chip(gated1)
    three0, two0, one0, own0 = out_proj(
        place, (gated0, _core(gated0), across0, _core(across0)), out_weight
    )
    three0 = _gx(three0, 1)
    one0 = _gx(one0, 1)
    joined0 = _add(two0, three0).astype(BF)
    two0 = _gx(joined0, 2)
    near1 = _core(across1)
    three1, two1, one1, own1 = out_proj(
        place, (gated1, _core(gated1), across1, near1), out_weight
    )
    three1 = _gx(three1, 1)
    one1 = _gx(one1, 1)
    two1 = _gx(_add(two1, three1).astype(BF), 2)
    return (
        jnp.concatenate([finish(own0, one0, two0), finish(own1, one1, two1)], axis=1),
        jnp.concatenate([next0, next1], axis=1),
        carry.reshape(ssm_state.shape),
    )


def per_device(
    normed,
    in_weight,
    conv_weight,
    conv_bias,
    x_weight,
    dt_weight,
    dt_bias,
    a_log,
    skip,
    conv_state,
    ssm_state,
    out_weight,
):
    a_rate = -jnp.exp(a_log)
    conv = conv_state
    state = ssm_state
    outputs = []
    for position in range(normed.shape[0]):
        partial_value = jnp.einsum(
            "rd,hde->rhe",
            lax.all_gather(normed[position], "gx", axis=1, tiled=True),
            in_weight,
            preferred_element_type=jnp.float32,
        )
        both_halves = lax.psum_scatter(
            partial_value.astype(jnp.bfloat16), "gy", scatter_dimension=2, tiled=True
        )
        inner_input = both_halves[:, 0, :]
        gate_input = both_halves[:, 1, :]
        accum = conv_bias[None, :] + conv_weight[CONV - 1][None, :] * inner_input.astype(
            jnp.float32
        )
        for tap in range(CONV - 1):
            accum = accum + conv_weight[tap][None, :] * conv[tap].astype(jnp.float32)
        conv_out = jax.nn.silu(accum).astype(jnp.bfloat16)
        conv = jnp.concatenate([conv[1:], inner_input[None]], axis=0)
        proj = lax.psum(
            jnp.dot(conv_out, x_weight, preferred_element_type=jnp.float32), ("gx", "gy")
        )
        step_low = proj[:, :DT].astype(jnp.bfloat16)
        b_in = proj[:, DT : DT + N]
        c_out = proj[:, DT + N :]
        delta = jax.nn.softplus(
            jnp.dot(step_low, dt_weight, preferred_element_type=jnp.float32) + dt_bias[None, :]
        )
        conv_float = conv_out.astype(jnp.float32)
        state = (
            jnp.exp(delta[:, None, :] * a_rate[None, :, :]) * state
            + delta[:, None, :] * b_in[:, :, None] * conv_float[:, None, :]
        )
        result = jnp.sum(c_out[:, :, None] * state, axis=1) + skip[None, :] * conv_float
        gated = (result * jax.nn.silu(gate_input.astype(jnp.float32))).astype(jnp.bfloat16)
        out_partial = jnp.dot(
            lax.all_gather(gated, "gy", axis=1, tiled=True),
            out_weight,
            preferred_element_type=jnp.float32,
        )
        outputs.append(
            lax.psum_scatter(
                out_partial.astype(jnp.bfloat16), "gx", scatter_dimension=1, tiled=True
            )
        )
    return (jnp.stack(outputs, axis=0), conv, state)


def solution(mesh):
    narrow = mesh.shape["gx"] == 4 and mesh.shape["gy"] == 4
    return jax.shard_map(
        chunked if narrow else per_device,
        mesh=mesh,
        in_specs=(
            P(None, "rep", ("gy", "gx")),
            P(None, "gy", "gx"),
            P(None, ("gx", "gy")),
            P(("gx", "gy")),
            P(("gx", "gy"), None),
            P(None, ("gx", "gy")),
            P(("gx", "gy")),
            P(None, ("gx", "gy")),
            P(("gx", "gy")),
            P(None, "rep", ("gx", "gy")),
            P("rep", None, ("gx", "gy")),
            P("gx", "gy"),
        ),
        out_specs=(
            P(None, "rep", ("gy", "gx")),
            P(None, "rep", ("gx", "gy")),
            P("rep", None, ("gx", "gy")),
        ),
        check_vma=False,
    )
```
